512 devices in a mesh: seq: 256 (over x, y, z), head: 2 (over core).
Axes of the slice: x: 4, y: 4, z: 16, core: 2. Of those that a mesh axis runs over, the one named last changes fastest.
Arguments:
- queries: bfloat16 [65536, 1024], P('seq', 'head'), may hold values from -6 to 6
- key_rows: bfloat16 [65536, 1024], P('seq', 'head'), may hold values from -6 to 6
- value_rows: bfloat16 [65536, 1024], P('seq', 'head'), may hold values from -6 to 6
- out_weight: bfloat16 [1024, 1024], P('head'), may hold values from -0.1875 to 0.1875
Outputs:
- layer_output: bfloat16 [65536, 1024], P('seq', 'head')
The draws below stay inside these ranges and needn't reach their ends.
All inputs are finite; a program needn't handle non-finite values.
Results may differ from the reference program's by a relative error of at most 0.015.
Values may be sent and summed in bfloat16 or wider, within the bound.
No kernel may reach another device: no remote copies, remote signals or barrier semaphores. Data moves between devices by JAX's collectives and lax.ppermute only.
A program may use at most 64 MiB of HBM per device.

```python
import math
from functools import reduce
import jax
import jax.numpy as jnp
from jax import lax

D = 1024
HEADS = 16
HEAD_DIM = 64
BLOCK = 128
LEVELS = 5
TOK_DEV = 256
TOKENS = 65536
N_HEAD = 2


def smooth_rough(key_in):
    rough_key, period_key, phase_key = jax.random.split(key_in, 3)
    rough = jax.random.truncated_normal(rough_key, -3.0, 3.0, (TOKENS, D), jnp.float32)
    periods = jnp.exp(jax.random.uniform(period_key, (1, D), jnp.float32, math.log(2.0 * BLOCK), math.log(8.0 * TOK_DEV)))
    phases = jax.random.uniform(phase_key, (1, D), jnp.float32, -math.pi, math.pi)
    position = jnp.arange(TOKENS, dtype=jnp.float32)[:, None]
    return rough + jnp.sin(2.0 * math.pi * position / periods + phases)


def draw_queries(key, part):
    key = jax.random.fold_in(key, 1)
    field = smooth_rough(key)
    return field.astype(jnp.bfloat16)


def draw_key_rows(key, part):
    key = jax.random.fold_in(key, 2)
    field = smooth_rough(key)
    return field.astype(jnp.bfloat16)


def draw_value_rows(key, part):
    key = jax.random.fold_in(key, 3)
    field = smooth_rough(key)
    return field.astype(jnp.bfloat16)


def shard_levels(own_key, dims, cuts, smallest, largest):
    loudness = 1.0
    for dim, blocks in cuts:
        heights = jax.random.uniform(jax.random.fold_in(jax.random.fold_in(own_key, 6), dim), (blocks,), jnp.float32, smallest / len(cuts), largest / len(cuts))
        loudness = loudness * jnp.repeat(jnp.exp(heights), dims[dim] // blocks).reshape((-1,) + (1,) * (len(dims) - 1 - dim))
    return loudness


def noise(key, extent, width, limit, cuts=(), kind=jnp.bfloat16):
    level = shard_levels(key, extent, cuts, -0.22, 0.18) if cuts else 1.0
    values = jax.random.normal(key, extent, jnp.float32) * width * level
    return jnp.minimum(jnp.maximum(values, -limit), limit).astype(kind)


def setup_inputs(seed: int = 0) -> dict:
    key_list = jax.random.split(jax.random.key(seed), 5)
    return {
        "queries": draw_queries(jax.random.fold_in(key_list[4], 71), 0),
        "key_rows": draw_key_rows(jax.random.fold_in(key_list[4], 71), 0),
        "value_rows": draw_value_rows(jax.random.fold_in(key_list[4], 71), 0),
        "out_weight": noise(key_list[3], (D, D), D ** -0.5, 0.1875, ((0, 2),)),
    }


def attend(query_blk, key_blk, value_blk):
    scores = jnp.einsum("nqe,nke->nqk", query_blk.astype(jnp.float32), key_blk.astype(jnp.float32)) * (HEAD_DIM ** -0.5)
    row_max = jnp.max(scores, axis=-1)
    weights = jnp.exp(scores - row_max[..., None])
    row_total = jnp.sum(weights, axis=-1)
    rounded = lax.optimization_barrier(weights.astype(jnp.bfloat16))
    weighted = jnp.einsum("nqk,nke->nqe", rounded.astype(jnp.float32), value_blk.astype(jnp.float32))
    return row_max.reshape(-1), row_total.reshape(-1), weighted.reshape(-1, HEAD_DIM)


def coarse(field, factor):
    merged = field.astype(jnp.float32).reshape(field.shape[0] // factor, factor, HEAD_DIM)
    return jnp.mean(merged, axis=1).astype(jnp.bfloat16)


def one_head(operands):
    query_one, key_one, value_one = operands
    length = query_one.shape[0]
    blocks_in = length // BLOCK
    terms = [(1, attend(query_one.reshape(blocks_in, BLOCK, HEAD_DIM), key_one.reshape(blocks_in, BLOCK, HEAD_DIM), value_one.reshape(blocks_in, BLOCK, HEAD_DIM)))]
    for depth_no in range(1, LEVELS + 1):
        factor = 2 ** (depth_no - 1)
        coarse_q = coarse(query_one, factor)
        coarse_k = coarse(key_one, factor)
        coarse_v = coarse(value_one, factor)
        pair_count = coarse_q.shape[0] // BLOCK
        query_blk = coarse_q.reshape(pair_count, BLOCK, HEAD_DIM)
        key_blk = coarse_k.reshape(pair_count // 2, 2, BLOCK, HEAD_DIM)[:, ::-1].reshape(pair_count, BLOCK, HEAD_DIM)
        value_blk = coarse_v.reshape(pair_count // 2, 2, BLOCK, HEAD_DIM)[:, ::-1].reshape(pair_count, BLOCK, HEAD_DIM)
        terms.append((factor, attend(query_blk, key_blk, value_blk)))
    spread = []
    for factor, (row_max, row_total, weighted) in terms:
        spread.append((factor, jnp.repeat(row_max, factor, axis=0), jnp.repeat(row_total, factor, axis=0), jnp.repeat(weighted, factor, axis=0)))
    highest = reduce(jnp.maximum, [entry[1] for entry in spread])
    denominator = jnp.zeros((length,), jnp.float32)
    numerator = jnp.zeros((length, HEAD_DIM), jnp.float32)
    for factor, row_max, row_total, weighted in spread:
        rescale = factor * jnp.exp(row_max - highest)
        denominator = denominator + rescale * row_total
        numerator = numerator + rescale[:, None] * weighted
    return (numerator / denominator[:, None]).astype(jnp.bfloat16)


def reference(queries, key_rows, value_rows, out_weight):
    length = queries.shape[0]

    def split_heads(field):
        return jnp.transpose(field.reshape(length, HEADS, HEAD_DIM), (1, 0, 2))

    per_head = lax.map(one_head, (split_heads(queries), split_heads(key_rows), split_heads(value_rows)))
    attention = jnp.transpose(per_head, (1, 0, 2)).reshape(length, D)
    group_cols = D // N_HEAD
    running = jnp.zeros((length, D), jnp.float32)
    for group_no in range(N_HEAD):
        partial_value = jnp.dot(attention[:, group_no * group_cols:(group_no + 1) * group_cols], out_weight[group_no * group_cols:(group_no + 1) * group_cols], preferred_element_type=jnp.float32).astype(jnp.bfloat16)
        partial_value = lax.optimization_barrier(partial_value)
        running = running + partial_value.astype(jnp.float32)
    return running.astype(jnp.bfloat16)
```

```python
import jax
import jax.numpy as jnp
from jax import lax
from jax.experimental import pallas as pl
from jax.experimental.pallas import tpu as pltpu
from jax.sharding import PartitionSpec as P

HEAD_DIM = 64
SCALE = 0.125
LANES = 128
RING = 16
VMEM_LIMIT = 16 * 1024 * 1024


def params(limit=VMEM_LIMIT):
    return pltpu.CompilerParams(vmem_limit_bytes=limit)


def half_lanes(shape):
    return lax.broadcasted_iota(jnp.int32, shape, 1) < HEAD_DIM


def attend_pair(query, key, value):
    rows = query.shape[0]
    scaled = query * jnp.bfloat16(SCALE)
    left = half_lanes(scaled.shape)
    zero = jnp.zeros_like(scaled)
    both = jnp.concatenate((jnp.where(left, scaled, zero), jnp.where(left, zero, scaled)), axis=0)
    scores = lax.dot_general(both, key, (((1,), (1,)), ((), ())), preferred_element_type=jnp.float32)
    row_max = jnp.max(scores, axis=1, keepdims=True)
    weights = jnp.exp(scores - row_max).astype(jnp.bfloat16)
    wide = jnp.concatenate((value, jnp.ones_like(value)), axis=1)
    sums = jnp.dot(weights, wide, preferred_element_type=jnp.float32)
    left = half_lanes((rows, LANES))
    highest = jnp.where(left, row_max[:rows], row_max[rows:])
    total = jnp.where(left, sums[:rows, LANES:], sums[rows:, LANES:])
    weighted = jnp.where(left, sums[:rows, :LANES], sums[rows:, :LANES])
    return highest, total, weighted


def merge(one, two, factor):
    highest = jnp.maximum(one[0], two[0])
    keep = jnp.exp(one[0] - highest)
    add = factor * jnp.exp(two[0] - highest)
    return highest, keep * one[1] + add * two[1], keep * one[2] + add * two[2]


def spread(ref, rows, factor):
    def run(value):
        for turn in range(factor):
            ref[pl.ds(turn, rows, stride=factor), :] = value
        return ref[pl.ds(0, rows * factor), :]

    return run


def mean_matrix(rows, shift):
    row = lax.broadcasted_iota(jnp.int32, (rows, rows << shift), 0)
    col = lax.broadcasted_iota(jnp.int32, (rows, rows << shift), 1)
    return jnp.where((col >> shift) == row, 1.0 / (1 << shift), 0.0).astype(jnp.bfloat16)


def coarse_kernel(q_hbm, k_hbm, v_hbm, q_ref, kv2_ref, kv3_ref, kv4_ref, kv5_ref, q_in, k_in, v_in, sems):
    copies = [
        pltpu.make_async_copy(hbm, vmem, sems.at[turn])
        for turn, (hbm, vmem) in enumerate(((k_hbm, k_in), (v_hbm, v_in), (q_hbm, q_in)))
    ]
    for copy in copies:
        copy.start()
    means = jnp.concatenate([mean_matrix(256 >> shift, shift) for shift in (1, 2, 3, 4)], axis=0)
    width = q_in.shape[1]
    for turn, field in enumerate((k_in, v_in)):
        copies[turn].wait()
        means_of = jnp.dot(means, field[...], preferred_element_type=jnp.float32).astype(jnp.bfloat16)
        cols = slice(turn * width, (turn + 1) * width)
        kv2_ref[:, cols] = means_of[:128]
        kv3_ref[:, cols] = means_of[128:192]
        kv4_ref[:, cols] = means_of[192:224]
        kv5_ref[:, cols] = means_of[224:240]
    copies[2].wait()
    q_ref[...] = jnp.dot(means, q_in[...], preferred_element_type=jnp.float32).astype(jnp.bfloat16)


def pack_kernel(kv4_ref, far5_ref, near5_ref, out_ref):
    out_ref[0:32, :] = kv4_ref[...]
    out_ref[32:48, :] = far5_ref[...]
    out_ref[48:64, :] = near5_ref[...]


def near_kernel(q_ref, k_ref, v_ref, top_ref, total_ref, sum_ref):
    for pair in range(4):
        cols = slice(pair * LANES, (pair + 1) * LANES)
        highest, total, weighted = attend_pair(q_ref[:, cols], k_ref[:, cols], v_ref[:, cols])
        top_ref[:, cols] = highest
        total_ref[:, cols] = total
        sum_ref[:, cols] = weighted


def middle_kernel(
    q_ref, kv2_ref, kv3a_ref, kv3b_ref, top_in, total_in, sum_in, top_ref, total_ref, sum_ref, scratch_ref
):
    width = q_ref.shape[1]
    for pair in range(4):
        cols = slice(pair * LANES, (pair + 1) * LANES)
        vcols = slice(width + pair * LANES, width + (pair + 1) * LANES)
        level2 = attend_pair(q_ref[:128, cols], kv2_ref[:, cols], kv2_ref[:, vcols])
        key3 = jnp.concatenate((kv3a_ref[:, cols], kv3b_ref[:, cols]), axis=0)
        value3 = jnp.concatenate((kv3a_ref[:, vcols], kv3b_ref[:, vcols]), axis=0)
        level3 = attend_pair(q_ref[128:192, cols], key3, value3)
        double = spread(scratch_ref, 64, 2)
        level2 = merge(level2, [double(part) for part in level3], 2.0)
        double = spread(scratch_ref, 128, 2)
        near = (top_in[:, cols], total_in[:, cols], sum_in[:, cols])
        top_ref[:, cols], total_ref[:, cols], sum_ref[:, cols] = merge(
            near, [double(part) for part in level2], 2.0
        )


def last_kernel(
    q_ref, one_ref, two_ref, three_ref, four_ref, top_ref, total_ref, sum_ref, w_ref, mine_ref, send_ref, scratch_ref
):
    core = lax.axis_index("head")
    width = q_ref.shape[1]
    parts = (one_ref, two_ref, three_ref, four_ref)
    pieces = []
    for pair in range(4):
        cols = slice(pair * LANES, (pair + 1) * LANES)
        vcols = slice(width + pair * LANES, width + (pair + 1) * LANES)
        key4, value4, key5, value5 = [
            jnp.concatenate([part[rows, lanes] for part in parts], axis=0)
            for rows in (slice(0, 32), slice(32, 64))
            for lanes in (cols, vcols)
        ]
        level4 = attend_pair(q_ref[192:224, cols], key4, value4)
        level5 = attend_pair(q_ref[224:240, cols], key5, value5)
        double = spread(scratch_ref, 16, 2)
        far = merge(level4, [double(part) for part in level5], 2.0)
        eight = spread(scratch_ref, 32, 8)
        near = (top_ref[:, cols], total_ref[:, cols], sum_ref[:, cols])
        near = merge(near, [eight(part) for part in far], 8.0)
        pieces.append((near[2] / near[1]).astype(jnp.bfloat16))
    attention = jnp.concatenate(pieces, axis=1)
    half = w_ref.shape[1] // 2
    away = pl.multiple_of((1 - core) * half, half)
    home = pl.multiple_of(core * half, half)
    send_ref[...] = jnp.dot(attention, w_ref[:, pl.ds(away, half)], preferred_element_type=jnp.float32).astype(
        jnp.bfloat16
    )
    mine_ref[...] = jnp.dot(attention, w_ref[:, pl.ds(home, half)], preferred_element_type=jnp.float32).astype(
        jnp.bfloat16
    )


def moved(block, partner):
    count = lax.axis_size("seq")
    return lax.ppermute(block, "seq", [(i, i - i % RING + partner(i % RING)) for i in range(count)])


def flip(mask):
    return lambda place: place ^ mask


def far_partner(place):
    return 11 - place if place // 4 in (0, 2) else 19 - place


def call(kernel, name, outs, scratch=(), flops=0, moved_bytes=1_000_000, exps=0, in_specs=None, limit=VMEM_LIMIT):
    given = {} if in_specs is None else {"in_specs": in_specs}
    return pl.pallas_call(
        kernel,
        out_shape=outs,
        scratch_shapes=list(scratch),
        compiler_params=params(limit),
        cost_estimate=pl.CostEstimate(flops=flops, bytes_accessed=moved_bytes, transcendentals=exps),
        name=name,
        **given,
    )


def body(queries, key_rows, value_rows, out_weight):
    rows, width = queries.shape
    f32, bf16 = jnp.float32, jnp.bfloat16
    shape = jax.ShapeDtypeStruct
    fields = (shape((rows, width), f32),) * 3
    coarse_q, kv2, kv3, kv4, kv5 = call(
        coarse_kernel,
        "coarse",
        (shape((240, width), bf16),) + tuple(shape((size, 2 * width), bf16) for size in (128, 64, 32, 16)),
        [pltpu.VMEM((rows, width), bf16)] * 3 + [pltpu.SemaphoreType.DMA((3,))],
        flops=2 * 240 * 256 * 1536,
        in_specs=[pl.BlockSpec(memory_space=pltpu.HBM)] * 3,
        limit=63 * 1024 * 1024,
    )(queries, key_rows, value_rows)
    far5 = moved(kv5, far_partner)
    far4 = moved(kv4, flip(4))
    near5 = moved(kv5, flip(12))
    kv3a = moved(kv3, flip(2))
    kv2_got = moved(kv2, flip(1))
    near = call(near_kernel, "near", fields, flops=8 * 256 * 256 * 64 * 4, exps=8 * 256 * 256)(
        queries, key_rows, value_rows
    )
    own = call(pack_kernel, "pack", shape((64, 2 * width), bf16))(far4, far5, near5)
    two = moved(own, flip(2))
    one = moved(own, flip(1))
    kv3b = moved(kv3a, flip(1))
    three = moved(two, flip(1))
    near = call(
        middle_kernel, "middle", fields, [pltpu.VMEM((256, LANES), f32)], flops=300_000_000, exps=8 * 256 * 200
    )(coarse_q, kv2_got, kv3a, kv3b, *near)
    mine, send = call(
        last_kernel,
        "last",
        (shape((rows, width), bf16),) * 2,
        [pltpu.VMEM((256, LANES), f32)],
        flops=600_000_000,
        exps=8 * 256 * 100,
    )(coarse_q, own, one, two, three, *near, out_weight)
    fetched = lax.ppermute(send, "head", [(0, 1), (1, 0)])
    return (mine.astype(f32) + fetched.astype(f32)).astype(bf16)


def solution(mesh):
    placed = (P("seq", "head"), P("seq", "head"), P("seq", "head"), P("head", None))
    return jax.shard_map(
        body, mesh=mesh, in_specs=placed, out_specs=P("seq", "head"), check_vma=False
    )
```

```python
import jax
import jax.numpy as jnp
from jax import lax
from jax.experimental import pallas as pl
from jax.experimental.pallas import tpu as pltpu
from jax.sharding import PartitionSpec as P

HEAD_DIM = 64
SCALE = 0.125
LANES = 128
RING = 16
NEVER = -1e30
VMEM_LIMIT = 16 * 1024 * 1024


def params(limit=VMEM_LIMIT):
    return pltpu.CompilerParams(vmem_limit_bytes=limit)


def half_lanes(shape):
    return lax.broadcasted_iota(jnp.int32, shape, 1) < HEAD_DIM


def attend_pair(query, key, value, pieces=False):
    rows = query.shape[0]
    scaled = query * jnp.bfloat16(SCALE)
    left = half_lanes(scaled.shape)
    zero = jnp.zeros_like(scaled)
    both = jnp.concatenate((jnp.where(left, scaled, zero), jnp.where(left, zero, scaled)), axis=0)
    scores = lax.dot_general(both, key, (((1,), (1,)), ((), ())), preferred_element_type=jnp.float32)
    if pieces:
        row = lax.broadcasted_iota(jnp.int32, scores.shape, 0)
        row = jnp.where(row >= rows, row - rows, row)
        col = lax.broadcasted_iota(jnp.int32, scores.shape, 1)
        scores = jnp.where((row < 32) == ((col & 63) < 32), scores, NEVER)
    row_max = jnp.max(scores, axis=1, keepdims=True)
    weights = jnp.exp(scores - row_max).astype(jnp.bfloat16)
    wide = jnp.concatenate((value, jnp.ones_like(value)), axis=1)
    sums = jnp.dot(weights, wide, preferred_element_type=jnp.float32)
    left = half_lanes((rows, LANES))
    highest = jnp.where(left, row_max[:rows], row_max[rows:])
    total = jnp.where(left, sums[:rows, LANES:], sums[rows:, LANES:])
    weighted = jnp.where(left, sums[:rows, :LANES], sums[rows:, :LANES])
    return highest, total, weighted


def merge(one, two, factor):
    highest = jnp.maximum(one[0], two[0])
    keep = jnp.exp(one[0] - highest)
    add = factor * jnp.exp(two[0] - highest)
    return highest, keep * one[1] + add * two[1], keep * one[2] + add * two[2]


def spread(ref, rows, factor):
    def run(value):
        for turn in range(factor):
            ref[pl.ds(turn, rows, stride=factor), :] = value
        return ref[pl.ds(0, rows * factor), :]

    return run


def mean_matrix(rows, shift):
    row = lax.broadcasted_iota(jnp.int32, (rows, rows << shift), 0)
    col = lax.broadcasted_iota(jnp.int32, (rows, rows << shift), 1)
    return jnp.where((col >> shift) == row, 1.0 / (1 << shift), 0.0).astype(jnp.bfloat16)


def coarse_kernel(q_hbm, k_hbm, v_hbm, q_ref, kv2_ref, kv3_ref, kv4_ref, kv5_ref, q_in, k_in, v_in, sems):
    copies = [
        pltpu.make_async_copy(hbm, vmem, sems.at[turn])
        for turn, (hbm, vmem) in enumerate(((k_hbm, k_in), (v_hbm, v_in), (q_hbm, q_in)))
    ]
    for copy in copies:
        copy.start()
    means = jnp.concatenate([mean_matrix(256 >> shift, shift) for shift in (1, 2, 3, 4)], axis=0)
    width = q_in.shape[1]
    for turn, field in enumerate((k_in, v_in)):
        copies[turn].wait()
        means_of = jnp.dot(means, field[...], preferred_element_type=jnp.float32).astype(jnp.bfloat16)
        cols = slice(turn * width, (turn + 1) * width)
        kv2_ref[:, cols] = means_of[:128]
        kv3_ref[:, cols] = means_of[128:192]
        kv4_ref[:, cols] = means_of[192:224]
        kv5_ref[:, cols] = means_of[224:240]
    copies[2].wait()
    q_ref[...] = jnp.dot(means, q_in[...], preferred_element_type=jnp.float32).astype(jnp.bfloat16)


def pack_kernel(kv4_ref, near5_ref, far5_ref, after3_ref, after2_ref, own_ref):
    own_ref[0:32, :] = kv4_ref[...]
    own_ref[32:48, :] = near5_ref[...]
    own_ref[48:64, :] = far5_ref[...]


def near_kernel(q_ref, k_ref, v_ref, top_ref, total_ref, sum_ref):
    for pair in range(4):
        cols = slice(pair * LANES, (pair + 1) * LANES)
        highest, total, weighted = attend_pair(q_ref[:, cols], k_ref[:, cols], v_ref[:, cols])
        top_ref[:, cols] = highest
        total_ref[:, cols] = total
        sum_ref[:, cols] = weighted


def middle_kernel(
    q_ref, kv2_ref, kv3a_ref, kv3b_ref, top_in, total_in, sum_in, top_ref, total_ref, sum_ref, scratch_ref
):
    width = q_ref.shape[1]
    for pair in range(4):
        cols = slice(pair * LANES, (pair + 1) * LANES)
        vcols = slice(width + pair * LANES, width + (pair + 1) * LANES)
        level2 = attend_pair(q_ref[:128, cols], kv2_ref[:, cols], kv2_ref[:, vcols])
        key3 = jnp.concatenate((kv3a_ref[:, cols], kv3b_ref[:, cols]), axis=0)
        value3 = jnp.concatenate((kv3a_ref[:, vcols], kv3b_ref[:, vcols]), axis=0)
        level3 = attend_pair(q_ref[128:192, cols], key3, value3)
        double = spread(scratch_ref, 64, 2)
        level2 = merge(level2, [double(part) for part in level3], 2.0)
        double = spread(scratch_ref, 128, 2)
        near = (top_in[:, cols], total_in[:, cols], sum_in[:, cols])
        top_ref[:, cols], total_ref[:, cols], sum_ref[:, cols] = merge(
            near, [double(part) for part in level2], 2.0
        )


def partial_kernel(q_ref, own_ref, one_ref, two_ref, top_ref, total_ref, sum_ref):
    width = q_ref.shape[1]
    parts = (own_ref, one_ref, two_ref)
    for pair in range(4):
        cols = slice(pair * LANES, (pair + 1) * LANES)
        vcols = slice(width + pair * LANES, width + (pair + 1) * LANES)
        key = jnp.concatenate([part[0:64, cols] for part in parts], axis=0)
        value = jnp.concatenate([part[0:64, vcols] for part in parts], axis=0)
        top_ref[:, cols], total_ref[:, cols], sum_ref[:, cols] = attend_pair(q_ref[192:240, cols], key, value, True)


def last_kernel(
    q_ref, part_ref, far_top, far_total, far_sum, top_ref, total_ref, sum_ref, w_ref, mine_ref, send_ref, *scratch
):
    core = lax.axis_index("head")
    width = q_ref.shape[1]
    pieces = []
    for pair in range(4):
        cols = slice(pair * LANES, (pair + 1) * LANES)
        vcols = slice(width + pair * LANES, width + (pair + 1) * LANES)
        piece = attend_pair(q_ref[192:240, cols], part_ref[:, cols], part_ref[:, vcols], True)
        far = merge((far_top[:, cols], far_total[:, cols], far_sum[:, cols]), piece, 1.0)
        level5 = [spread(ref, 16, 2)(part[32:48]) for ref, part in zip(scratch[6 * pair :], far)]
        level4 = merge([part[0:32] for part in far], level5, 2.0)
        far = [spread(ref, 32, 8)(part) for ref, part in zip(scratch[6 * pair + 3 :], level4)]
        near = merge((top_ref[:, cols], total_ref[:, cols], sum_ref[:, cols]), far, 8.0)
        pieces.append((near[2] / near[1]).astype(jnp.bfloat16))
    attention = jnp.concatenate(pieces, axis=1)
    half = w_ref.shape[1] // 2
    away = pl.multiple_of((1 - core) * half, half)
    home = pl.multiple_of(core * half, half)
    send_ref[...] = jnp.dot(attention, w_ref[:, pl.ds(away, half)], preferred_element_type=jnp.float32).astype(
        jnp.bfloat16
    )
    mine_ref[...] = jnp.dot(attention, w_ref[:, pl.ds(home, half)], preferred_element_type=jnp.float32).astype(
        jnp.bfloat16
    )


def moved(block, partner):
    count = lax.axis_size("seq")
    return lax.ppermute(block, "seq", [(i, i - i % RING + partner(i % RING)) for i in range(count)])


def flip(mask):
    return lambda place: place ^ mask


def far_partner(place):
    return 11 - place if place // 4 in (0, 2) else 19 - place


def call(kernel, name, outs, scratch=(), flops=0, moved_bytes=1_000_000, exps=0, limit=VMEM_LIMIT, **more):
    return pl.pallas_call(
        kernel,
        out_shape=outs,
        scratch_shapes=list(scratch),
        compiler_params=params(limit),
        cost_estimate=pl.CostEstimate(flops=flops, bytes_accessed=moved_bytes, transcendentals=exps),
        name=name,
        **more,
    )


def body(queries, key_rows, value_rows, out_weight):
    rows, width = queries.shape
    f32, bf16 = jnp.float32, jnp.bfloat16
    shape = jax.ShapeDtypeStruct
    fields = (shape((rows, width), f32),) * 3
    coarse_q, kv2, kv3, kv4, kv5 = call(
        coarse_kernel,
        "coarse",
        (shape((240, width), bf16),) + tuple(shape((size, 2 * width), bf16) for size in (128, 64, 32, 16)),
        [pltpu.VMEM((rows, width), bf16)] * 3 + [pltpu.SemaphoreType.DMA((3,))],
        flops=2 * 240 * 256 * 1536,
        in_specs=[pl.BlockSpec(memory_space=pltpu.HBM)] * 3,
        limit=63 * 1024 * 1024,
    )(queries, key_rows, value_rows)
    far4 = moved(kv4, flip(4))
    near5 = moved(kv5, flip(12))
    far5 = moved(kv5, far_partner)
    kv3a = moved(kv3, flip(2))
    kv2_got = moved(kv2, flip(1))
    near = call(near_kernel, "near", fields, flops=8 * 256 * 256 * 64 * 4, exps=8 * 256 * 256)(
        queries, key_rows, value_rows
    )
    whole, anywhere = pl.BlockSpec(memory_space=pltpu.VMEM), pl.BlockSpec(memory_space=pl.ANY)
    own = call(
        pack_kernel,
        "pack",
        shape((64, 2 * width), bf16),
        in_specs=(whole, whole, whole, anywhere, anywhere),
    )(far4, near5, far5, kv3a, kv2_got)
    two = moved(own, flip(2))
    one = moved(own, flip(1))
    kv3b = moved(kv3a, flip(1))
    three = moved(two, flip(1))
    near = call(
        middle_kernel, "middle", fields, [pltpu.VMEM((256, LANES), f32)], flops=300_000_000, exps=8 * 256 * 200
    )(coarse_q, kv2_got, kv3a, kv3b, *near)
    far = call(partial_kernel, "partial", (shape((48, width), f32),) * 3, flops=60_000_000, exps=8 * 48 * 192)(
        coarse_q, own, one, two
    )
    mine, send = call(
        last_kernel,
        "last",
        (shape((rows, width), bf16),) * 2,
        ([pltpu.VMEM((32, LANES), f32)] * 3 + [pltpu.VMEM((256, LANES), f32)] * 3) * 4,
        flops=600_000_000,
        exps=8 * 256 * 100,
    )(coarse_q, three, *far, *near, out_weight)
    fetched = lax.ppermute(send, "head", [(0, 1), (1, 0)])
    return (mine.astype(f32) + fetched.astype(f32)).astype(bf16)


def solution(mesh):
    placed = (P("seq", "head"), P("seq", "head"), P("seq", "head"), P("head", None))
    return jax.shard_map(
        body, mesh=mesh, in_specs=placed, out_specs=P("seq", "head"), check_vma=False
    )
```

```python
import jax
import jax.numpy as jnp
from jax import lax
from jax.experimental import pallas as pl
from jax.experimental.pallas import tpu as pltpu
from jax.sharding import PartitionSpec as P

HEAD_DIM = 64
SCALE = 0.125
LANES = 128
RING = 16
NEVER = -1e30
VMEM_LIMIT = 16 * 1024 * 1024


def params(limit=VMEM_LIMIT):
    return pltpu.CompilerParams(vmem_limit_bytes=limit)


def half_lanes(shape):
    return lax.broadcasted_iota(jnp.int32, shape, 1) < HEAD_DIM


def attend_pair(query, key, value, pieces=False):
    rows = query.shape[0]
    scaled = query * jnp.bfloat16(SCALE)
    left = half_lanes(scaled.shape)
    zero = jnp.zeros_like(scaled)
    both = jnp.concatenate((jnp.where(left, scaled, zero), jnp.where(left, zero, scaled)), axis=0)
    scores = lax.dot_general(both, key, (((1,), (1,)), ((), ())), preferred_element_type=jnp.float32)
    if pieces:
        row = lax.broadcasted_iota(jnp.int32, scores.shape, 0)
        row = jnp.where(row >= rows, row - rows, row)
        col = lax.broadcasted_iota(jnp.int32, scores.shape, 1)
        scores = jnp.where((row < 32) == ((col & 63) < 32), scores, NEVER)
    row_max = jnp.max(scores, axis=1, keepdims=True)
    weights = jnp.exp(scores - row_max).astype(jnp.bfloat16)
    wide = jnp.concatenate((value, jnp.ones_like(value)), axis=1)
    sums = jnp.dot(weights, wide, preferred_element_type=jnp.float32)
    left = half_lanes((rows, LANES))
    highest = jnp.where(left, row_max[:rows], row_max[rows:])
    total = jnp.where(left, sums[:rows, LANES:], sums[rows:, LANES:])
    weighted = jnp.where(left, sums[:rows, :LANES], sums[rows:, :LANES])
    return highest, total, weighted


def merge(one, two, factor):
    highest = jnp.maximum(one[0], two[0])
    keep = jnp.exp(one[0] - highest)
    add = factor * jnp.exp(two[0] - highest)
    return highest, keep * one[1] + add * two[1], keep * one[2] + add * two[2]


def spread(ref, rows, factor):
    def run(value):
        for turn in range(factor):
            ref[pl.ds(turn, rows, stride=factor), :] = value
        return ref[pl.ds(0, rows * factor), :]

    return run


def mean_matrix(rows, shift):
    row = lax.broadcasted_iota(jnp.int32, (rows, rows << shift), 0)
    col = lax.broadcasted_iota(jnp.int32, (rows, rows << shift), 1)
    return jnp.where((col >> shift) == row, 1.0 / (1 << shift), 0.0).astype(jnp.bfloat16)


def coarse_kernel(q_hbm, k_hbm, v_hbm, q_ref, kv2_ref, kv3_ref, kv4_ref, kv5_ref, q_in, k_in, v_in, sems):
    copies = [
        pltpu.make_async_copy(hbm, vmem, sems.at[turn])
        for turn, (hbm, vmem) in enumerate(((k_hbm, k_in), (v_hbm, v_in), (q_hbm, q_in)))
    ]
    for copy in copies:
        copy.start()
    means = jnp.concatenate([mean_matrix(256 >> shift, shift) for shift in (1, 2, 3, 4)], axis=0)
    width = q_in.shape[1]
    for turn, field in enumerate((k_in, v_in)):
        copies[turn].wait()
        means_of = jnp.dot(means, field[...], preferred_element_type=jnp.float32).astype(jnp.bfloat16)
        cols = slice(turn * width, (turn + 1) * width)
        kv2_ref[:, cols] = means_of[:128]
        kv3_ref[:, cols] = means_of[128:192]
        kv4_ref[:, cols] = means_of[192:224]
        kv5_ref[:, cols] = means_of[224:240]
    copies[2].wait()
    q_ref[...] = jnp.dot(means, q_in[...], preferred_element_type=jnp.float32).astype(jnp.bfloat16)


def pack_kernel(kv4_ref, near5_ref, far5_ref, out_ref):
    out_ref[0:32, :] = kv4_ref[...]
    out_ref[32:48, :] = near5_ref[...]
    out_ref[48:64, :] = far5_ref[...]


def near_kernel(q_ref, k_ref, v_ref, top_ref, total_ref, sum_ref):
    for pair in range(4):
        cols = slice(pair * LANES, (pair + 1) * LANES)
        highest, total, weighted = attend_pair(q_ref[:, cols], k_ref[:, cols], v_ref[:, cols])
        top_ref[:, cols] = highest
        total_ref[:, cols] = total
        sum_ref[:, cols] = weighted


def middle_kernel(
    q_ref, kv2_ref, kv3a_ref, kv3b_ref, top_in, total_in, sum_in, top_ref, total_ref, sum_ref, scratch_ref
):
    width = q_ref.shape[1]
    for pair in range(4):
        cols = slice(pair * LANES, (pair + 1) * LANES)
        vcols = slice(width + pair * LANES, width + (pair + 1) * LANES)
        level2 = attend_pair(q_ref[:128, cols], kv2_ref[:, cols], kv2_ref[:, vcols])
        key3 = jnp.concatenate((kv3a_ref[:, cols], kv3b_ref[:, cols]), axis=0)
        value3 = jnp.concatenate((kv3a_ref[:, vcols], kv3b_ref[:, vcols]), axis=0)
        level3 = attend_pair(q_ref[128:192, cols], key3, value3)
        double = spread(scratch_ref, 64, 2)
        level2 = merge(level2, [double(part) for part in level3], 2.0)
        double = spread(scratch_ref, 128, 2)
        near = (top_in[:, cols], total_in[:, cols], sum_in[:, cols])
        top_ref[:, cols], total_ref[:, cols], sum_ref[:, cols] = merge(
            near, [double(part) for part in level2], 2.0
        )


def partial_kernel(q_ref, own_ref, one_ref, two_ref, top_ref, total_ref, sum_ref):
    width = q_ref.shape[1]
    parts = (own_ref, one_ref, two_ref)
    for pair in range(4):
        cols = slice(pair * LANES, (pair + 1) * LANES)
        vcols = slice(width + pair * LANES, width + (pair + 1) * LANES)
        key = jnp.concatenate([part[:, cols] for part in parts], axis=0)
        value = jnp.concatenate([part[:, vcols] for part in parts], axis=0)
        top_ref[:, cols], total_ref[:, cols], sum_ref[:, cols] = attend_pair(q_ref[192:240, cols], key, value, True)


def last_kernel(
    q_ref, part_ref, far_top, far_total, far_sum, top_ref, total_ref, sum_ref, w_ref, attention_ref, send_ref, *scratch
):
    core = lax.axis_index("head")
    width = q_ref.shape[1]
    pieces = []
    for pair in range(4):
        cols = slice(pair * LANES, (pair + 1) * LANES)
        vcols = slice(width + pair * LANES, width + (pair + 1) * LANES)
        piece = attend_pair(q_ref[192:240, cols], part_ref[:, cols], part_ref[:, vcols], True)
        far = merge((far_top[:, cols], far_total[:, cols], far_sum[:, cols]), piece, 1.0)
        level5 = [spread(ref, 16, 2)(part[32:48]) for ref, part in zip(scratch[6 * pair :], far)]
        level4 = merge([part[0:32] for part in far], level5, 2.0)
        far = [spread(ref, 32, 8)(part) for ref, part in zip(scratch[6 * pair + 3 :], level4)]
        near = merge((top_ref[:, cols], total_ref[:, cols], sum_ref[:, cols]), far, 8.0)
        pieces.append((near[2] / near[1]).astype(jnp.bfloat16))
    attention = jnp.concatenate(pieces, axis=1)
    attention_ref[...] = attention
    half = w_ref.shape[1] // 2
    away = pl.multiple_of((1 - core) * half, half)
    send_ref[...] = jnp.dot(attention, w_ref[:, pl.ds(away, half)], preferred_element_type=jnp.float32).astype(
        jnp.bfloat16
    )


def mine_kernel(attention_ref, w_ref, mine_ref):
    half = w_ref.shape[1] // 2
    home = pl.multiple_of(lax.axis_index("head") * half, half)
    mine_ref[...] = jnp.dot(
        attention_ref[...], w_ref[:, pl.ds(home, half)], preferred_element_type=jnp.float32
    ).astype(jnp.bfloat16)


def moved(block, partner):
    count = lax.axis_size("seq")
    return lax.ppermute(block, "seq", [(i, i - i % RING + partner(i % RING)) for i in range(count)])


def flip(mask):
    return lambda place: place ^ mask


def far_partner(place):
    return 11 - place if place // 4 in (0, 2) else 19 - place


def call(kernel, name, outs, scratch=(), flops=0, moved_bytes=1_000_000, exps=0, in_specs=None, limit=VMEM_LIMIT):
    given = {} if in_specs is None else {"in_specs": in_specs}
    return pl.pallas_call(
        kernel,
        out_shape=outs,
        scratch_shapes=list(scratch),
        compiler_params=params(limit),
        cost_estimate=pl.CostEstimate(flops=flops, bytes_accessed=moved_bytes, transcendentals=exps),
        name=name,
        **given,
    )


def body(queries, key_rows, value_rows, out_weight):
    rows, width = queries.shape
    f32, bf16 = jnp.float32, jnp.bfloat16
    shape = jax.ShapeDtypeStruct
    fields = (shape((rows, width), f32),) * 3
    coarse_q, kv2, kv3, kv4, kv5 = call(
        coarse_kernel,
        "coarse",
        (shape((240, width), bf16),) + tuple(shape((size, 2 * width), bf16) for size in (128, 64, 32, 16)),
        [pltpu.VMEM((rows, width), bf16)] * 3 + [pltpu.SemaphoreType.DMA((3,))],
        flops=2 * 240 * 256 * 1536,
        in_specs=[pl.BlockSpec(memory_space=pltpu.HBM)] * 3,
        limit=63 * 1024 * 1024,
    )(queries, key_rows, value_rows)
    far4 = moved(kv4, flip(4))
    near5 = moved(kv5, flip(12))
    far5 = moved(kv5, far_partner)
    kv3a = moved(kv3, flip(2))
    kv2_got = moved(kv2, flip(1))
    near = call(near_kernel, "near", fields, flops=8 * 256 * 256 * 64 * 4, exps=8 * 256 * 256)(
        queries, key_rows, value_rows
    )
    own = call(pack_kernel, "pack", shape((64, 2 * width), bf16))(far4, near5, far5)
    two = moved(own, flip(2))
    one = moved(own, flip(1))
    kv3b = moved(kv3a, flip(1))
    three = moved(two, flip(1))
    near = call(
        middle_kernel, "middle", fields, [pltpu.VMEM((256, LANES), f32)], flops=300_000_000, exps=8 * 256 * 200
    )(coarse_q, kv2_got, kv3a, kv3b, *near)
    far = call(partial_kernel, "partial", (shape((48, width), f32),) * 3, flops=60_000_000, exps=8 * 48 * 192)(
        coarse_q, own, one, two
    )
    attention, send = call(
        last_kernel,
        "last",
        (shape((rows, width), bf16),) * 2,
        ([pltpu.VMEM((32, LANES), f32)] * 3 + [pltpu.VMEM((256, LANES), f32)] * 3) * 4,
        flops=600_000_000,
        exps=8 * 256 * 100,
    )(coarse_q, three, *far, *near, out_weight)
    fetched = lax.ppermute(send, "head", [(0, 1), (1, 0)])
    mine = call(mine_kernel, "mine", shape((rows, width), bf16), flops=2 * 256 * 512 * 512)(attention, out_weight)
    return (mine.astype(f32) + fetched.astype(f32)).astype(bf16)


def solution(mesh):
    placed = (P("seq", "head"), P("seq", "head"), P("seq", "head"), P("head", None))
    return jax.shard_map(
        body, mesh=mesh, in_specs=placed, out_specs=P("seq", "head"), check_vma=False
    )
```

```python
import jax
import jax.numpy as jnp
from jax import lax
from jax.experimental import pallas as pl
from jax.experimental.pallas import tpu as pltpu
from jax.sharding import PartitionSpec as P

HEAD_DIM = 64
SCALE = 0.125
LANES = 128
RING = 16
NEVER = -1e30
VMEM_LIMIT = 16 * 1024 * 1024


def params(limit=VMEM_LIMIT):
    return pltpu.CompilerParams(vmem_limit_bytes=limit)


def half_lanes(shape):
    return lax.broadcasted_iota(jnp.int32, shape, 1) < HEAD_DIM


def attend_pair(query, key, value, pieces=False):
    rows = query.shape[0]
    scaled = query * jnp.bfloat16(SCALE)
    left = half_lanes(scaled.shape)
    zero = jnp.zeros_like(scaled)
    both = jnp.concatenate((jnp.where(left, scaled, zero), jnp.where(left, zero, scaled)), axis=0)
    scores = lax.dot_general(both, key, (((1,), (1,)), ((), ())), preferred_element_type=jnp.float32)
    if pieces:
        row = lax.broadcasted_iota(jnp.int32, scores.shape, 0)
        row = jnp.where(row >= rows, row - rows, row)
        col = lax.broadcasted_iota(jnp.int32, scores.shape, 1)
        scores = jnp.where((row < 32) == ((col & 63) < 32), scores, NEVER)
    row_max = jnp.max(scores, axis=1, keepdims=True)
    weights = jnp.exp(scores - row_max).astype(jnp.bfloat16)
    wide = jnp.concatenate((value, jnp.ones_like(value)), axis=1)
    sums = jnp.dot(weights, wide, preferred_element_type=jnp.float32)
    left = half_lanes((rows, LANES))
    highest = jnp.where(left, row_max[:rows], row_max[rows:])
    total = jnp.where(left, sums[:rows, LANES:], sums[rows:, LANES:])
    weighted = jnp.where(left, sums[:rows, :LANES], sums[rows:, :LANES])
    return highest, total, weighted


def merge(one, two, factor):
    highest = jnp.maximum(one[0], two[0])
    keep = jnp.exp(one[0] - highest)
    add = factor * jnp.exp(two[0] - highest)
    return highest, keep * one[1] + add * two[1], keep * one[2] + add * two[2]


def spread(ref, rows, factor):
    def run(value):
        for turn in range(factor):
            ref[pl.ds(turn, rows, stride=factor), :] = value
        return ref[pl.ds(0, rows * factor), :]

    return run


def mean_matrix(rows, shift):
    row = lax.broadcasted_iota(jnp.int32, (rows, rows << shift), 0)
    col = lax.broadcasted_iota(jnp.int32, (rows, rows << shift), 1)
    return jnp.where((col >> shift) == row, 1.0 / (1 << shift), 0.0).astype(jnp.bfloat16)


def coarse_kernel(k_hbm, v_hbm, kv2_ref, kv3_ref, kv4_ref, kv5_ref, k_in, v_in, sems):
    copies = [
        pltpu.make_async_copy(hbm, vmem, sems.at[turn])
        for turn, (hbm, vmem) in enumerate(((k_hbm, k_in), (v_hbm, v_in)))
    ]
    for copy in copies:
        copy.start()
    means = jnp.concatenate([mean_matrix(256 >> shift, shift) for shift in (1, 2, 3, 4)], axis=0)
    width = k_in.shape[1]
    for turn, field in enumerate((k_in, v_in)):
        copies[turn].wait()
        means_of = jnp.dot(means, field[...], preferred_element_type=jnp.float32).astype(jnp.bfloat16)
        cols = slice(turn * width, (turn + 1) * width)
        kv2_ref[:, cols] = means_of[:128]
        kv3_ref[:, cols] = means_of[128:192]
        kv4_ref[:, cols] = means_of[192:224]
        kv5_ref[:, cols] = means_of[224:240]


def query_kernel(q_ref, coarse_ref):
    means = jnp.concatenate([mean_matrix(256 >> shift, shift) for shift in (1, 2, 3, 4)], axis=0)
    coarse_ref[...] = jnp.dot(means, q_ref[...], preferred_element_type=jnp.float32).astype(jnp.bfloat16)


def pack_kernel(kv4_ref, near5_ref, far5_ref, out_ref):
    out_ref[0:32, :] = kv4_ref[...]
    out_ref[32:48, :] = near5_ref[...]
    out_ref[48:64, :] = far5_ref[...]


def pack_near_kernel(own_ref, kv3_ref, out_ref):
    out_ref[0:64, :] = own_ref[...]
    out_ref[64:128, :] = kv3_ref[...]


def near_kernel(q_ref, k_ref, v_ref, top_ref, total_ref, sum_ref):
    for pair in range(4):
        cols = slice(pair * LANES, (pair + 1) * LANES)
        highest, total, weighted = attend_pair(q_ref[:, cols], k_ref[:, cols], v_ref[:, cols])
        top_ref[:, cols] = highest
        total_ref[:, cols] = total
        sum_ref[:, cols] = weighted


def middle_kernel(
    q_ref, kv2_ref, kv3a_ref, one_ref, top_in, total_in, sum_in, top_ref, total_ref, sum_ref, scratch_ref
):
    width = q_ref.shape[1]
    for pair in range(4):
        cols = slice(pair * LANES, (pair + 1) * LANES)
        vcols = slice(width + pair * LANES, width + (pair + 1) * LANES)
        level2 = attend_pair(q_ref[:128, cols], kv2_ref[:, cols], kv2_ref[:, vcols])
        key3 = jnp.concatenate((kv3a_ref[:, cols], one_ref[64:128, cols]), axis=0)
        value3 = jnp.concatenate((kv3a_ref[:, vcols], one_ref[64:128, vcols]), axis=0)
        level3 = attend_pair(q_ref[128:192, cols], key3, value3)
        double = spread(scratch_ref, 64, 2)
        level2 = merge(level2, [double(part) for part in level3], 2.0)
        double = spread(scratch_ref, 128, 2)
        near = (top_in[:, cols], total_in[:, cols], sum_in[:, cols])
        top_ref[:, cols], total_ref[:, cols], sum_ref[:, cols] = merge(
            near, [double(part) for part in level2], 2.0
        )


def partial_kernel(q_ref, own_ref, one_ref, two_ref, top_ref, total_ref, sum_ref):
    width = q_ref.shape[1]
    parts = (own_ref, one_ref, two_ref)
    for pair in range(4):
        cols = slice(pair * LANES, (pair + 1) * LANES)
        vcols = slice(width + pair * LANES, width + (pair + 1) * LANES)
        key = jnp.concatenate([part[0:64, cols] for part in parts], axis=0)
        value = jnp.concatenate([part[0:64, vcols] for part in parts], axis=0)
        top_ref[:, cols], total_ref[:, cols], sum_ref[:, cols] = attend_pair(q_ref[192:240, cols], key, value, True)


def last_kernel(
    q_ref, part_ref, far_top, far_total, far_sum, top_ref, total_ref, sum_ref, w_ref, attention_ref, send_ref, *scratch
):
    core = lax.axis_index("head")
    width = q_ref.shape[1]
    pieces = []
    for pair in range(4):
        cols = slice(pair * LANES, (pair + 1) * LANES)
        vcols = slice(width + pair * LANES, width + (pair + 1) * LANES)
        piece = attend_pair(q_ref[192:240, cols], part_ref[:, cols], part_ref[:, vcols], True)
        far = merge((far_top[:, cols], far_total[:, cols], far_sum[:, cols]), piece, 1.0)
        level5 = [spread(ref, 16, 2)(part[32:48]) for ref, part in zip(scratch[6 * pair :], far)]
        level4 = merge([part[0:32] for part in far], level5, 2.0)
        far = [spread(ref, 32, 8)(part) for ref, part in zip(scratch[6 * pair + 3 :], level4)]
        near = merge((top_ref[:, cols], total_ref[:, cols], sum_ref[:, cols]), far, 8.0)
        pieces.append((near[2] / near[1]).astype(jnp.bfloat16))
    attention = jnp.concatenate(pieces, axis=1)
    attention_ref[...] = attention
    half = w_ref.shape[1] // 2
    away = pl.multiple_of((1 - core) * half, half)
    send_ref[...] = jnp.dot(attention, w_ref[:, pl.ds(away, half)], preferred_element_type=jnp.float32).astype(
        jnp.bfloat16
    )


def mine_kernel(attention_ref, w_ref, mine_ref):
    half = w_ref.shape[1] // 2
    home = pl.multiple_of(lax.axis_index("head") * half, half)
    mine_ref[...] = jnp.dot(
        attention_ref[...], w_ref[:, pl.ds(home, half)], preferred_element_type=jnp.float32
    ).astype(jnp.bfloat16)


def moved(block, partner):
    count = lax.axis_size("seq")
    return lax.ppermute(block, "seq", [(i, i - i % RING + partner(i % RING)) for i in range(count)])


def flip(mask):
    return lambda place: place ^ mask


def far_partner(place):
    return 11 - place if place // 4 in (0, 2) else 19 - place


def call(kernel, name, outs, scratch=(), flops=0, moved_bytes=1_000_000, exps=0, in_specs=None, limit=VMEM_LIMIT):
    given = {} if in_specs is None else {"in_specs": in_specs}
    return pl.pallas_call(
        kernel,
        out_shape=outs,
        scratch_shapes=list(scratch),
        compiler_params=params(limit),
        cost_estimate=pl.CostEstimate(flops=flops, bytes_accessed=moved_bytes, transcendentals=exps),
        name=name,
        **given,
    )


def body(queries, key_rows, value_rows, out_weight):
    rows, width = queries.shape
    f32, bf16 = jnp.float32, jnp.bfloat16
    shape = jax.ShapeDtypeStruct
    fields = (shape((rows, width), f32),) * 3
    kv2, kv3, kv4, kv5 = call(
        coarse_kernel,
        "coarse",
        tuple(shape((size, 2 * width), bf16) for size in (128, 64, 32, 16)),
        [pltpu.VMEM((rows, width), bf16)] * 2 + [pltpu.SemaphoreType.DMA((2,))],
        flops=2 * 240 * 256 * 1024,
        in_specs=[pl.BlockSpec(memory_space=pltpu.HBM)] * 2,
        limit=63 * 1024 * 1024,
    )(key_rows, value_rows)
    coarse_q = call(query_kernel, "queries", shape((240, width), bf16), flops=2 * 240 * 256 * 512)(queries)
    far4 = moved(kv4, flip(4))
    near5 = moved(kv5, flip(12))
    far5 = moved(kv5, far_partner)
    kv3a = moved(kv3, flip(2))
    kv2_got = moved(kv2, flip(1))
    near = call(near_kernel, "near", fields, flops=8 * 256 * 256 * 64 * 4, exps=8 * 256 * 256)(
        queries, key_rows, value_rows
    )
    own = call(pack_kernel, "pack", shape((64, 2 * width), bf16))(far4, near5, far5)
    two = moved(own, flip(2))
    both = call(pack_near_kernel, "pack_near", shape((128, 2 * width), bf16))(own, kv3a)
    one = moved(both, flip(1))
    three = moved(two, flip(1))
    near = call(
        middle_kernel, "middle", fields, [pltpu.VMEM((256, LANES), f32)], flops=300_000_000, exps=8 * 256 * 200
    )(coarse_q, kv2_got, kv3a, one, *near)
    far = call(partial_kernel, "partial", (shape((48, width), f32),) * 3, flops=60_000_000, exps=8 * 48 * 192)(
        coarse_q, own, one, two
    )
    attention, send = call(
        last_kernel,
        "last",
        (shape((rows, width), bf16),) * 2,
        ([pltpu.VMEM((32, LANES), f32)] * 3 + [pltpu.VMEM((256, LANES), f32)] * 3) * 4,
        flops=600_000_000,
        exps=8 * 256 * 100,
    )(coarse_q, three, *far, *near, out_weight)
    fetched = lax.ppermute(send, "head", [(0, 1), (1, 0)])
    mine = call(mine_kernel, "mine", shape((rows, width), bf16), flops=2 * 256 * 512 * 512)(attention, out_weight)
    return (mine.astype(f32) + fetched.astype(f32)).astype(bf16)


def solution(mesh):
    placed = (P("seq", "head"), P("seq", "head"), P("seq", "head"), P("head", None))
    return jax.shard_map(
        body, mesh=mesh, in_specs=placed, out_specs=P("seq", "head"), check_vma=False
    )
```

```python
import jax
import jax.numpy as jnp
from jax import lax
from jax.experimental import pallas as pl
from jax.experimental.pallas import tpu as pltpu
from jax.sharding import PartitionSpec as P

HEAD_DIM = 64
SCALE = 0.125
LANES = 128
RING = 16
NEVER = -1e30
VMEM_LIMIT = 16 * 1024 * 1024


def params(limit=VMEM_LIMIT):
    return pltpu.CompilerParams(vmem_limit_bytes=limit)


def half_lanes(shape):
    return lax.broadcasted_iota(jnp.int32, shape, 1) < HEAD_DIM


def attend_pair(query, key, value, pieces=False):
    rows = query.shape[0]
    scaled = query * jnp.bfloat16(SCALE)
    left = half_lanes(scaled.shape)
    zero = jnp.zeros_like(scaled)
    both = jnp.concatenate((jnp.where(left, scaled, zero), jnp.where(left, zero, scaled)), axis=0)
    scores = lax.dot_general(both, key, (((1,), (1,)), ((), ())), preferred_element_type=jnp.float32)
    if pieces:
        row = lax.broadcasted_iota(jnp.int32, scores.shape, 0)
        row = jnp.where(row >= rows, row - rows, row)
        col = lax.broadcasted_iota(jnp.int32, scores.shape, 1)
        scores = jnp.where((row < 32) == ((col & 63) < 32), scores, NEVER)
    row_max = jnp.max(scores, axis=1, keepdims=True)
    weights = jnp.exp(scores - row_max).astype(jnp.bfloat16)
    wide = jnp.concatenate((value, jnp.ones_like(value)), axis=1)
    sums = jnp.dot(weights, wide, preferred_element_type=jnp.float32)
    left = half_lanes((rows, LANES))
    highest = jnp.where(left, row_max[:rows], row_max[rows:])
    total = jnp.where(left, sums[:rows, LANES:], sums[rows:, LANES:])
    weighted = jnp.where(left, sums[:rows, :LANES], sums[rows:, :LANES])
    return highest, total, weighted


def merge(one, two, factor):
    highest = jnp.maximum(one[0], two[0])
    keep = jnp.exp(one[0] - highest)
    add = factor * jnp.exp(two[0] - highest)
    return highest, keep * one[1] + add * two[1], keep * one[2] + add * two[2]


def spread(ref, rows, factor):
    def run(value):
        for turn in range(factor):
            ref[pl.ds(turn, rows, stride=factor), :] = value
        return ref[pl.ds(0, rows * factor), :]

    return run


def mean_matrix(rows, shift):
    row = lax.broadcasted_iota(jnp.int32, (rows, rows << shift), 0)
    col = lax.broadcasted_iota(jnp.int32, (rows, rows << shift), 1)
    return jnp.where((col >> shift) == row, 1.0 / (1 << shift), 0.0).astype(jnp.bfloat16)


def coarse_kernel(k_hbm, v_hbm, *rest):
    outs, held, (k_in, v_in, in_sems, out_sems) = rest[:4], rest[4:8], rest[8:]
    rows, width = k_in.shape
    half = rows // 2
    loads = []
    for turn, (hbm, vmem) in enumerate(((k_hbm, k_in), (v_hbm, v_in))):
        for part in range(2):
            place = pl.ds(part * half, half)
            loads.append(pltpu.make_async_copy(hbm.at[place], vmem.at[place], in_sems.at[2 * turn + part]))
    for load in loads:
        load.start()
    means = jnp.concatenate([mean_matrix(256 >> shift, shift) for shift in (1, 2, 3, 4)], axis=0)
    stores = []
    for turn, field in enumerate((k_in, v_in)):
        loads[2 * turn].wait()
        loads[2 * turn + 1].wait()
        means_of = jnp.dot(means, field[...], preferred_element_type=jnp.float32).astype(jnp.bfloat16)
        cols = pl.ds(turn * width, width)
        for level, (first, size) in enumerate(((0, 128), (128, 64), (192, 32), (224, 16))):
            held[level][:, cols] = means_of[first : first + size]
            store = pltpu.make_async_copy(
                held[level].at[:, cols], outs[level].at[:, cols], out_sems.at[4 * turn + level]
            )
            store.start()
            stores.append(store)
    for store in stores:
        store.wait()


def query_kernel(q_ref, coarse_ref):
    means = jnp.concatenate([mean_matrix(256 >> shift, shift) for shift in (1, 2, 3, 4)], axis=0)
    coarse_ref[...] = jnp.dot(means, q_ref[...], preferred_element_type=jnp.float32).astype(jnp.bfloat16)


def pack_kernel(kv4_ref, near5_ref, far5_ref, out_ref):
    out_ref[0:32, :] = kv4_ref[...]
    out_ref[32:48, :] = near5_ref[...]
    out_ref[48:64, :] = far5_ref[...]


def near_kernel(q_ref, k_ref, v_ref, top_ref, total_ref, sum_ref):
    for pair in range(4):
        cols = slice(pair * LANES, (pair + 1) * LANES)
        highest, total, weighted = attend_pair(q_ref[:, cols], k_ref[:, cols], v_ref[:, cols])
        top_ref[:, cols] = highest
        total_ref[:, cols] = total
        sum_ref[:, cols] = weighted


def middle_kernel(
    q_ref, kv2_ref, kv3a_ref, kv3b_ref, top_in, total_in, sum_in, top_ref, total_ref, sum_ref, scratch_ref
):
    width = q_ref.shape[1]
    for pair in range(4):
        cols = slice(pair * LANES, (pair + 1) * LANES)
        vcols = slice(width + pair * LANES, width + (pair + 1) * LANES)
        level2 = attend_pair(q_ref[:128, cols], kv2_ref[:, cols], kv2_ref[:, vcols])
        key3 = jnp.concatenate((kv3a_ref[:, cols], kv3b_ref[:, cols]), axis=0)
        value3 = jnp.concatenate((kv3a_ref[:, vcols], kv3b_ref[:, vcols]), axis=0)
        level3 = attend_pair(q_ref[128:192, cols], key3, value3)
        double = spread(scratch_ref, 64, 2)
        level2 = merge(level2, [double(part) for part in level3], 2.0)
        double = spread(scratch_ref, 128, 2)
        near = (top_in[:, cols], total_in[:, cols], sum_in[:, cols])
        top_ref[:, cols], total_ref[:, cols], sum_ref[:, cols] = merge(
            near, [double(part) for part in level2], 2.0
        )


def partial_kernel(q_ref, own_ref, one_ref, two_ref, top_ref, total_ref, sum_ref):
    width = q_ref.shape[1]
    parts = (own_ref, one_ref, two_ref)
    for pair in range(4):
        cols = slice(pair * LANES, (pair + 1) * LANES)
        vcols = slice(width + pair * LANES, width + (pair + 1) * LANES)
        key = jnp.concatenate([part[:, cols] for part in parts], axis=0)
        value = jnp.concatenate([part[:, vcols] for part in parts], axis=0)
        top_ref[:, cols], total_ref[:, cols], sum_ref[:, cols] = attend_pair(q_ref[192:240, cols], key, value, True)


def last_kernel(
    q_ref, part_ref, far_top, far_total, far_sum, top_ref, total_ref, sum_ref, w_ref, attention_ref, send_ref, *scratch
):
    core = lax.axis_index("head")
    width = q_ref.shape[1]
    pieces = []
    for pair in range(4):
        cols = slice(pair * LANES, (pair + 1) * LANES)
        vcols = slice(width + pair * LANES, width + (pair + 1) * LANES)
        piece = attend_pair(q_ref[192:240, cols], part_ref[:, cols], part_ref[:, vcols], True)
        far = merge((far_top[:, cols], far_total[:, cols], far_sum[:, cols]), piece, 1.0)
        level5 = [spread(ref, 16, 2)(part[32:48]) for ref, part in zip(scratch[6 * pair :], far)]
        level4 = merge([part[0:32] for part in far], level5, 2.0)
        far = [spread(ref, 32, 8)(part) for ref, part in zip(scratch[6 * pair + 3 :], level4)]
        near = merge((top_ref[:, cols], total_ref[:, cols], sum_ref[:, cols]), far, 8.0)
        pieces.append((near[2] / near[1]).astype(jnp.bfloat16))
    attention = jnp.concatenate(pieces, axis=1)
    attention_ref[...] = attention
    half = w_ref.shape[1] // 2
    away = pl.multiple_of((1 - core) * half, half)
    send_ref[...] = jnp.dot(attention, w_ref[:, pl.ds(away, half)], preferred_element_type=jnp.float32).astype(
        jnp.bfloat16
    )


def mine_kernel(attention_ref, w_ref, mine_ref):
    half = w_ref.shape[1] // 2
    home = pl.multiple_of(lax.axis_index("head") * half, half)
    mine_ref[...] = jnp.dot(
        attention_ref[...], w_ref[:, pl.ds(home, half)], preferred_element_type=jnp.float32
    ).astype(jnp.bfloat16)


def moved(block, partner):
    count = lax.axis_size("seq")
    return lax.ppermute(block, "seq", [(i, i - i % RING + partner(i % RING)) for i in range(count)])


def flip(mask):
    return lambda place: place ^ mask


def far_partner(place):
    return 11 - place if place // 4 in (0, 2) else 19 - place


def call(kernel, name, outs, scratch=(), flops=0, moved_bytes=1_000_000, exps=0, limit=VMEM_LIMIT, **given):
    return pl.pallas_call(
        kernel,
        out_shape=outs,
        scratch_shapes=list(scratch),
        compiler_params=params(limit),
        cost_estimate=pl.CostEstimate(flops=flops, bytes_accessed=moved_bytes, transcendentals=exps),
        name=name,
        **given,
    )


def body(queries, key_rows, value_rows, out_weight):
    rows, width = queries.shape
    f32, bf16 = jnp.float32, jnp.bfloat16
    shape = jax.ShapeDtypeStruct
    fields = (shape((rows, width), f32),) * 3
    sizes = (128, 64, 32, 16)
    hbm = pl.BlockSpec(memory_space=pltpu.HBM)
    kv2, kv3, kv4, kv5 = call(
        coarse_kernel,
        "coarse",
        tuple(shape((size, 2 * width), bf16) for size in sizes),
        [pltpu.VMEM((size, 2 * width), bf16) for size in sizes]
        + [pltpu.VMEM((rows, width), bf16)] * 2
        + [pltpu.SemaphoreType.DMA((4,)), pltpu.SemaphoreType.DMA((8,))],
        flops=2 * 240 * 256 * 1024,
        in_specs=(hbm, hbm),
        out_specs=(hbm,) * 4,
        limit=63 * 1024 * 1024,
    )(key_rows, value_rows)
    coarse_q = call(query_kernel, "queries", shape((240, width), bf16), flops=2 * 240 * 256 * 512)(queries)
    far4 = moved(kv4, flip(4))
    near5 = moved(kv5, flip(12))
    far5 = moved(kv5, far_partner)
    kv3a = moved(kv3, flip(2))
    kv2_got = moved(kv2, flip(1))
    near = call(near_kernel, "near", fields, flops=8 * 256 * 256 * 64 * 4, exps=8 * 256 * 256)(
        queries, key_rows, value_rows
    )
    own = call(pack_kernel, "pack", shape((64, 2 * width), bf16))(far4, near5, far5)
    two = moved(own, flip(2))
    one = moved(own, flip(1))
    kv3b = moved(kv3a, flip(1))
    three = moved(two, flip(1))
    near = call(
        middle_kernel, "middle", fields, [pltpu.VMEM((256, LANES), f32)], flops=300_000_000, exps=8 * 256 * 200
    )(coarse_q, kv2_got, kv3a, kv3b, *near)
    far = call(partial_kernel, "partial", (shape((48, width), f32),) * 3, flops=60_000_000, exps=8 * 48 * 192)(
        coarse_q, own, one, two
    )
    attention, send = call(
        last_kernel,
        "last",
        (shape((rows, width), bf16),) * 2,
        ([pltpu.VMEM((32, LANES), f32)] * 3 + [pltpu.VMEM((256, LANES), f32)] * 3) * 4,
        flops=600_000_000,
        exps=8 * 256 * 100,
    )(coarse_q, three, *far, *near, out_weight)
    fetched = lax.ppermute(send, "head", [(0, 1), (1, 0)])
    mine = call(mine_kernel, "mine", shape((rows, width), bf16), flops=2 * 256 * 512 * 512)(attention, out_weight)
    return (mine.astype(f32) + fetched.astype(f32)).astype(bf16)


def solution(mesh):
    placed = (P("seq", "head"), P("seq", "head"), P("seq", "head"), P("head", None))
    return jax.shard_map(
        body, mesh=mesh, in_specs=placed, out_specs=P("seq", "head"), check_vma=False
    )
```

```python
import jax
import jax.numpy as jnp
from jax import lax
from jax.experimental import pallas as pl
from jax.experimental.pallas import tpu as pltpu
from jax.sharding import PartitionSpec as P

HEAD_DIM = 64
SCALE = 0.125
LANES = 128
RING = 16
NEVER = -1e30
VMEM_LIMIT = 16 * 1024 * 1024


def params(limit=VMEM_LIMIT):
    return pltpu.CompilerParams(vmem_limit_bytes=limit)


def half_lanes(shape):
    return lax.broadcasted_iota(jnp.int32, shape, 1) < HEAD_DIM


def attend_pair(query, key, value, pieces=False):
    rows = query.shape[0]
    scaled = query * jnp.bfloat16(SCALE)
    left = half_lanes(scaled.shape)
    zero = jnp.zeros_like(scaled)
    both = jnp.concatenate((jnp.where(left, scaled, zero), jnp.where(left, zero, scaled)), axis=0)
    scores = lax.dot_general(both, key, (((1,), (1,)), ((), ())), preferred_element_type=jnp.float32)
    if pieces:
        row = lax.broadcasted_iota(jnp.int32, scores.shape, 0)
        row = jnp.where(row >= rows, row - rows, row)
        col = lax.broadcasted_iota(jnp.int32, scores.shape, 1)
        scores = jnp.where((row < 32) == ((col & 63) < 32), scores, NEVER)
    row_max = jnp.max(scores, axis=1, keepdims=True)
    weights = jnp.exp(scores - row_max).astype(jnp.bfloat16)
    wide = jnp.concatenate((value, jnp.ones_like(value)), axis=1)
    sums = jnp.dot(weights, wide, preferred_element_type=jnp.float32)
    left = half_lanes((rows, LANES))
    highest = jnp.where(left, row_max[:rows], row_max[rows:])
    total = jnp.where(left, sums[:rows, LANES:], sums[rows:, LANES:])
    weighted = jnp.where(left, sums[:rows, :LANES], sums[rows:, :LANES])
    return highest, total, weighted


def merge(one, two, factor):
    highest = jnp.maximum(one[0], two[0])
    keep = jnp.exp(one[0] - highest)
    add = factor * jnp.exp(two[0] - highest)
    return highest, keep * one[1] + add * two[1], keep * one[2] + add * two[2]


def spread(ref, rows, factor):
    def run(value):
        for turn in range(factor):
            ref[pl.ds(turn, rows, stride=factor), :] = value
        return ref[pl.ds(0, rows * factor), :]

    return run


def mean_matrix(rows, shift):
    row = lax.broadcasted_iota(jnp.int32, (rows, rows << shift), 0)
    col = lax.broadcasted_iota(jnp.int32, (rows, rows << shift), 1)
    return jnp.where((col >> shift) == row, 1.0 / (1 << shift), 0.0).astype(jnp.bfloat16)


def coarse_kernel(q_hbm, k_hbm, v_hbm, q_ref, kv2_ref, kv3_ref, kv4_ref, kv5_ref, q_in, k_in, v_in, sems):
    copies = [
        pltpu.make_async_copy(hbm, vmem, sems.at[turn])
        for turn, (hbm, vmem) in enumerate(((k_hbm, k_in), (v_hbm, v_in), (q_hbm, q_in)))
    ]
    for copy in copies:
        copy.start()
    means = jnp.concatenate([mean_matrix(256 >> shift, shift) for shift in (1, 2, 3, 4)], axis=0)
    width = q_in.shape[1]
    for turn, field in enumerate((k_in, v_in)):
        copies[turn].wait()
        means_of = jnp.dot(means, field[...], preferred_element_type=jnp.float32).astype(jnp.bfloat16)
        cols = slice(turn * width, (turn + 1) * width)
        kv2_ref[:, cols] = means_of[:128]
        kv3_ref[:, cols] = means_of[128:192]
        kv4_ref[:, cols] = means_of[192:224]
        kv5_ref[:, cols] = means_of[224:240]
    copies[2].wait()
    q_ref[...] = jnp.dot(means, q_in[...], preferred_element_type=jnp.float32).astype(jnp.bfloat16)


def pack_kernel(kv4_ref, near5_ref, far5_ref, after_ref, out_ref):
    out_ref[0:32, :] = kv4_ref[...]
    out_ref[32:48, :] = near5_ref[...]
    out_ref[48:64, :] = far5_ref[...]


def near_kernel(q_ref, k_ref, v_ref, top_ref, total_ref, sum_ref):
    for pair in range(4):
        cols = slice(pair * LANES, (pair + 1) * LANES)
        highest, total, weighted = attend_pair(q_ref[:, cols], k_ref[:, cols], v_ref[:, cols])
        top_ref[:, cols] = highest
        total_ref[:, cols] = total
        sum_ref[:, cols] = weighted


def middle_kernel(
    q_ref, kv2_ref, kv3a_ref, kv3b_ref, top_in, total_in, sum_in, top_ref, total_ref, sum_ref, scratch_ref
):
    width = q_ref.shape[1]
    for pair in range(4):
        cols = slice(pair * LANES, (pair + 1) * LANES)
        vcols = slice(width + pair * LANES, width + (pair + 1) * LANES)
        level2 = attend_pair(q_ref[:128, cols], kv2_ref[:, cols], kv2_ref[:, vcols])
        key3 = jnp.concatenate((kv3a_ref[:, cols], kv3b_ref[:, cols]), axis=0)
        value3 = jnp.concatenate((kv3a_ref[:, vcols], kv3b_ref[:, vcols]), axis=0)
        level3 = attend_pair(q_ref[128:192, cols], key3, value3)
        double = spread(scratch_ref, 64, 2)
        level2 = merge(level2, [double(part) for part in level3], 2.0)
        double = spread(scratch_ref, 128, 2)
        near = (top_in[:, cols], total_in[:, cols], sum_in[:, cols])
        top_ref[:, cols], total_ref[:, cols], sum_ref[:, cols] = merge(
            near, [double(part) for part in level2], 2.0
        )


def partial_kernel(q_ref, own_ref, one_ref, two_ref, top_ref, total_ref, sum_ref):
    width = q_ref.shape[1]
    parts = (own_ref, one_ref, two_ref)
    for pair in range(4):
        cols = slice(pair * LANES, (pair + 1) * LANES)
        vcols = slice(width + pair * LANES, width + (pair + 1) * LANES)
        key = jnp.concatenate([part[:, cols] for part in parts], axis=0)
        value = jnp.concatenate([part[:, vcols] for part in parts], axis=0)
        top_ref[:, cols], total_ref[:, cols], sum_ref[:, cols] = attend_pair(q_ref[192:240, cols], key, value, True)


def last_kernel(
    q_ref, part_ref, far_top, far_total, far_sum, top_ref, total_ref, sum_ref, w_ref, attention_ref, send_ref, *scratch
):
    core = lax.axis_index("head")
    width = q_ref.shape[1]
    pieces = []
    for pair in range(4):
        cols = slice(pair * LANES, (pair + 1) * LANES)
        vcols = slice(width + pair * LANES, width + (pair + 1) * LANES)
        piece = attend_pair(q_ref[192:240, cols], part_ref[:, cols], part_ref[:, vcols], True)
        far = merge((far_top[:, cols], far_total[:, cols], far_sum[:, cols]), piece, 1.0)
        level5 = [spread(ref, 16, 2)(part[32:48]) for ref, part in zip(scratch[6 * pair :], far)]
        level4 = merge([part[0:32] for part in far], level5, 2.0)
        far = [spread(ref, 32, 8)(part) for ref, part in zip(scratch[6 * pair + 3 :], level4)]
        near = merge((top_ref[:, cols], total_ref[:, cols], sum_ref[:, cols]), far, 8.0)
        pieces.append((near[2] / near[1]).astype(jnp.bfloat16))
    attention = jnp.concatenate(pieces, axis=1)
    attention_ref[...] = attention
    half = w_ref.shape[1] // 2
    away = pl.multiple_of((1 - core) * half, half)
    send_ref[...] = jnp.dot(attention, w_ref[:, pl.ds(away, half)], preferred_element_type=jnp.float32).astype(
        jnp.bfloat16
    )


def mine_kernel(attention_ref, w_ref, mine_ref):
    half = w_ref.shape[1] // 2
    home = pl.multiple_of(lax.axis_index("head") * half, half)
    mine_ref[...] = jnp.dot(
        attention_ref[...], w_ref[:, pl.ds(home, half)], preferred_element_type=jnp.float32
    ).astype(jnp.bfloat16)


def moved(block, partner):
    count = lax.axis_size("seq")
    return lax.ppermute(block, "seq", [(i, i - i % RING + partner(i % RING)) for i in range(count)])


def flip(mask):
    return lambda place: place ^ mask


def far_partner(place):
    return 11 - place if place // 4 in (0, 2) else 19 - place


def call(kernel, name, outs, scratch=(), flops=0, moved_bytes=1_000_000, exps=0, in_specs=None, limit=VMEM_LIMIT):
    given = {} if in_specs is None else {"in_specs": in_specs}
    return pl.pallas_call(
        kernel,
        out_shape=outs,
        scratch_shapes=list(scratch),
        compiler_params=params(limit),
        cost_estimate=pl.CostEstimate(flops=flops, bytes_accessed=moved_bytes, transcendentals=exps),
        name=name,
        **given,
    )


def body(queries, key_rows, value_rows, out_weight):
    rows, width = queries.shape
    f32, bf16 = jnp.float32, jnp.bfloat16
    shape = jax.ShapeDtypeStruct
    fields = (shape((rows, width), f32),) * 3
    coarse_q, kv2, kv3, kv4, kv5 = call(
        coarse_kernel,
        "coarse",
        (shape((240, width), bf16),) + tuple(shape((size, 2 * width), bf16) for size in (128, 64, 32, 16)),
        [pltpu.VMEM((rows, width), bf16)] * 3 + [pltpu.SemaphoreType.DMA((3,))],
        flops=2 * 240 * 256 * 1536,
        in_specs=[pl.BlockSpec(memory_space=pltpu.HBM)] * 3,
        limit=63 * 1024 * 1024,
    )(queries, key_rows, value_rows)
    far4 = moved(kv4, flip(4))
    near5 = moved(kv5, flip(12))
    far5 = moved(kv5, far_partner)
    kv3a = moved(kv3, flip(2))
    kv2_got = moved(kv2, flip(1))
    near = call(near_kernel, "near", fields, flops=8 * 256 * 256 * 64 * 4, exps=8 * 256 * 256)(
        queries, key_rows, value_rows
    )
    whole, anywhere = pl.BlockSpec(memory_space=pltpu.VMEM), pl.BlockSpec(memory_space=pl.ANY)
    own = call(
        pack_kernel, "pack", shape((64, 2 * width), bf16), in_specs=(whole, whole, whole, anywhere)
    )(far4, near5, far5, near[0])
    two = moved(own, flip(2))
    one = moved(own, flip(1))
    kv3b = moved(kv3a, flip(1))
    three = moved(two, flip(1))
    near = call(
        middle_kernel, "middle", fields, [pltpu.VMEM((256, LANES), f32)], flops=300_000_000, exps=8 * 256 * 200
    )(coarse_q, kv2_got, kv3a, kv3b, *near)
    far = call(partial_kernel, "partial", (shape((48, width), f32),) * 3, flops=60_000_000, exps=8 * 48 * 192)(
        coarse_q, own, one, two
    )
    attention, send = call(
        last_kernel,
        "last",
        (shape((rows, width), bf16),) * 2,
        ([pltpu.VMEM((32, LANES), f32)] * 3 + [pltpu.VMEM((256, LANES), f32)] * 3) * 4,
        flops=600_000_000,
        exps=8 * 256 * 100,
    )(coarse_q, three, *far, *near, out_weight)
    fetched = lax.ppermute(send, "head", [(0, 1), (1, 0)])
    mine = call(mine_kernel, "mine", shape((rows, width), bf16), flops=2 * 256 * 512 * 512)(attention, out_weight)
    return (mine.astype(f32) + fetched.astype(f32)).astype(bf16)


def solution(mesh):
    placed = (P("seq", "head"), P("seq", "head"), P("seq", "head"), P("head", None))
    return jax.shard_map(
        body, mesh=mesh, in_specs=placed, out_specs=P("seq", "head"), check_vma=False
    )
```
